32 devices in a mesh: groups: 2 (over x), samples: 16 (over z, y, core).
Axes of the slice: x: 2, y: 2, z: 4, core: 2. Of those that a mesh axis runs over, the one named last changes fastest.
Arguments:
- energies: float32 [256, 393216], P(None, ('groups', 'samples')), parts along dimension 1, may hold values from -700 to 700
- mult: int32 [393216, 256], P(('groups', 'samples')), parts along dimension 0, may hold values from 0 to 3
- state_counts: int32 [512], P('groups'), parts along dimension 0, may hold values from 1 to 1536, 196608 in all
Outputs:
- free_energy: float32 [512, 256], P('groups'), parts along dimension 0
The draws below stay inside these ranges and needn't reach their ends.
There are 2 independent parts, one for each index of `groups`. The reference program is written for one: setup_inputs(seed, part) draws one part's arguments, and reference() takes and returns one part's arrays. A program takes and returns all parts, laid end to end along the dimension named above; each array names one. Nothing has to cross between parts.
All inputs are finite; a program needn't handle non-finite values.
Results may differ from the reference program's by a relative error of at most 0.0003.
Values sent between devices are 32-bit elements; how exact they have to be, the bound alone decides.
A program may use at most 128 MiB of HBM per device.

```python
import math
import jax
import jax.numpy as jnp
import numpy as np
from jax import lax

STATES = 256
REPS = 256
ITERS = 4
SAMP_DEV = 12288
SAMPLES = 196608
N_SAMPLES = 16


def draw_energies(key, part):
    key_base = jax.random.fold_in(key, 11)
    key_noise = jax.random.fold_in(key, 12)
    key_home = jax.random.fold_in(key, 14)
    key_width = jax.random.fold_in(key, 15)
    coupled = jnp.arange(STATES, dtype=jnp.float32)[:, None] / (STATES - 1)
    position = jnp.arange(SAMPLES, dtype=jnp.int32)[None, :]
    jitter = jax.random.uniform(key_home, (1, SAMPLES), jnp.float32, 0.0, 1.0)
    home = (position.astype(jnp.float32) + jitter) / SAMPLES
    base = jax.random.uniform(key_base, (1, SAMPLES), jnp.float32, -400.0, 400.0)
    spread = jnp.clip(jax.random.normal(key_width, (1, SAMPLES), jnp.float32), -4.0, 4.0)
    noise = jnp.clip(jax.random.normal(key_noise, (STATES, SAMPLES), jnp.float32), -3.0, 3.0)
    coupling = 98.0 - 196.0 * home + 14.0 * spread
    base = jnp.where(position == 0, 720.0, jnp.where(position == 1, -720.0, base))
    energy = base + coupled * coupling + noise
    return jnp.clip(energy, -700.0, 700.0).astype(jnp.float32)


def draw_mult(key, part):
    key_block = jax.random.fold_in(key, 21)
    key_pick = jax.random.fold_in(key, 22)
    key_single = jax.random.fold_in(key, 23)
    position = jnp.arange(SAMPLES, dtype=jnp.int32)
    run_index = position * 32 // SAMPLES
    block_values = jax.random.randint(key_block, (32, REPS), 0, 4, jnp.int32)
    blocked = block_values[run_index]
    single = jax.random.randint(key_single, (SAMPLES, REPS), 0, 4, jnp.int32)
    picker = jax.random.randint(key_pick, (SAMPLES, REPS), 0, 4, jnp.int32)
    result = jnp.where(picker == 0, single, blocked)
    replicate = jnp.arange(REPS, dtype=jnp.int32)[None, :]
    column = position[:, None]
    result = jnp.where((column == 0) & (replicate == 0), 3, result)
    result = jnp.where((column == 1) & (replicate == 0), 0, result)
    return result.astype(jnp.int32)


def profile(amount, total, reach, slope):
    portions = [(1 << 20) // math.isqrt(grade ** slope) + 1 for grade in range(2, amount + 1)]
    surplus, counts = total - reach - (amount - 1), [1] * (amount - 1)
    while surplus > 0:
        movable = [i for i in range(amount - 1) if counts[i] < reach]
        mass, left = sum([portions[i] for i in movable]), surplus
        for i in movable:
            addition = min(reach - counts[i], max(1, left * portions[i] // mass), surplus)
            counts[i] = counts[i] + addition
            surplus = surplus - addition
    return np.array([reach] + counts)


def uneven_parts(own_key, number_of, total, reach, slope):
    if number_of == 2:
        one = jax.random.randint(own_key, (), max(1, total - reach), min(reach, total - 1) + 1)
        return jnp.stack([one, total - one])
    lengths = jnp.asarray(profile(number_of, total, reach, slope), jnp.int32)
    pairs = (number_of - 1) // 2
    giver, receiver = lengths[1:1 + 2 * pairs:2], lengths[2:2 + 2 * pairs:2]
    margin = jnp.minimum(giver - 1, reach - receiver)
    shifted = jax.random.randint(jax.random.fold_in(own_key, 1), (pairs,), 0, 1 << 20) % (margin + 1)
    lengths = lengths.at[1:1 + 2 * pairs:2].set(giver - shifted).at[2:2 + 2 * pairs:2].set(receiver + shifted)
    return lengths[jax.random.permutation(jax.random.fold_in(own_key, 2), number_of)]


def setup_inputs(seed: int = 0, part: int = 0) -> dict:
    key_list = jax.random.split(jax.random.key(seed), 4)
    own_keys = jax.random.split(jax.random.fold_in(key_list[3], part), 4)
    return {
        "energies": draw_energies(jax.random.fold_in(jax.random.fold_in(key_list[3], part), 71), part),
        "mult": draw_mult(jax.random.fold_in(jax.random.fold_in(key_list[3], part), 71), part),
        "state_counts": uneven_parts(own_keys[2], STATES, SAMPLES, 2 * SAMPLES // STATES, 2).astype(jnp.int32),
    }


def reference(energies, mult, state_counts):
    counts_f = state_counts.astype(jnp.float32)[:, None]
    free = jnp.zeros((STATES, REPS), jnp.float32)

    def numer_of(weight):
        def add_block(index, total):
            start = (index * SAMP_DEV).astype(jnp.int32)
            block = lax.dynamic_slice_in_dim(energies, start, SAMP_DEV, 1)
            mblock = lax.dynamic_slice_in_dim(mult, start, SAMP_DEV, 0)
            shift = jnp.min(block, axis=0, keepdims=True)
            boltz = jnp.exp(shift - block).astype(jnp.bfloat16)
            denom = jnp.dot(boltz.T, weight, preferred_element_type=jnp.float32)
            ratio = (mblock.astype(jnp.float32) / denom).astype(jnp.bfloat16)
            return total + jnp.dot(boltz, ratio, preferred_element_type=jnp.float32)

        return lax.fori_loop(0, N_SAMPLES, add_block, jnp.zeros((STATES, REPS), jnp.float32))

    for step in range(ITERS):
        weight = (counts_f * jnp.exp(free)).astype(jnp.bfloat16)
        logs = jnp.log(numer_of(weight))
        free = logs[0:1] - logs
    return free
```

```python
import functools

import jax
import jax.numpy as jnp
from jax import lax
from jax.experimental import pallas as pl
from jax.experimental.pallas import tpu as pltpu
from jax.sharding import PartitionSpec as P

ITERS = 4
CHUNK = 1024


def mbar_kernel(num_dev, counts_ref, e_hbm, m_hbm, out_ref, e_buf, m_buf, bz, bzt, weight,
                counts, acc, half, core_recv, part_recv, gathered,
                e_sem, m_sem, core_sem, part_send, part_sem, gat_send, gat_sem, fwd_send, fwd_sem):
    states, reps = acc.shape
    samples = e_buf.shape[1]
    chunks = samples // CHUNK
    chips = num_dev // 2
    hrows = states // 2
    prows = hrows // chips
    me = lax.axis_index("samples")
    chip, core = me // 2, lax.rem(me, 2)
    other = 1 - core

    def device(chip_at, core_at):
        return {"samples": chip_at * 2 + core_at}

    def chip_ahead(d):
        return lax.rem(chip + d, chips)

    def chip_behind(d):
        return lax.rem(chip + (chips - d), chips)

    def e_copy(i):
        cols = pl.ds(pl.multiple_of(i * CHUNK, CHUNK), CHUNK)
        return pltpu.make_async_copy(e_hbm.at[:, cols], e_buf.at[:, cols], e_sem.at[i])

    def m_copy(i):
        rows = pl.ds(pl.multiple_of(i * CHUNK, CHUNK), CHUNK)
        return pltpu.make_async_copy(m_hbm.at[rows, :], m_buf.at[rows, :], m_sem.at[i])

    @pl.loop(0, chunks)
    def _(i):
        e_copy(i).start()
        m_copy(i).start()

    barrier = pltpu.get_barrier_semaphore()
    pl.semaphore_signal(barrier, inc=1, device_id=device(chip, other))
    for d in range(1, chips):
        pl.semaphore_signal(barrier, inc=1, device_id=device(chip_ahead(d), core))

    counts[...] = jnp.broadcast_to(counts_ref[...].astype(jnp.float32), (reps, states)).T
    weight[...] = counts[...].astype(jnp.bfloat16)

    def terms(i, boltz, boltz_t):
        rows = pl.ds(pl.multiple_of(i * CHUNK, CHUNK), CHUNK)
        denom = jnp.dot(boltz_t, weight[...], preferred_element_type=jnp.float32)
        ratio = (m_buf[rows, :].astype(jnp.float32) / denom).astype(jnp.bfloat16)
        acc[...] += jnp.dot(boltz, ratio, preferred_element_type=jnp.float32)

    def all_reduce(t):
        def to_core(rows, sem):
            return pltpu.make_async_remote_copy(
                src_ref=acc.at[rows], dst_ref=core_recv.at[t],
                send_sem=core_sem.at[t, 0], recv_sem=core_sem.at[t, 1],
                device_id=device(chip, other))

        core_copy = to_core(pl.ds(pl.multiple_of(other * hrows, hrows), hrows), core_sem)
        core_copy.start()
        core_copy.wait_recv()

        def part_of(at):
            return pl.ds(pl.multiple_of(at * prows, prows), prows)

        def row_of(core_at, chip_at):
            return pl.ds(pl.multiple_of(core_at * hrows + chip_at * prows, prows), prows)

        sends = [core_copy]
        part_copies = []
        for d in range(1, chips):
            to = chip_ahead(d)
            half[t, part_of(to), :] = acc[row_of(core, to), :] + core_recv[t, part_of(to), :]
            copy = pltpu.make_async_remote_copy(
                src_ref=half.at[t, part_of(to)], dst_ref=part_recv.at[t, d - 1],
                send_sem=part_send.at[t, d - 1], recv_sem=part_sem.at[t, d - 1],
                device_id=device(to, core))
            copy.start()
            part_copies.append(copy)
        total = acc[row_of(core, chip), :] + core_recv[t, part_of(chip), :]
        for d in range(1, chips):
            part_copies[d - 1].wait_recv()
            total = total + part_recv[t, d - 1]
        mine = row_of(core, chip)
        gathered[t, mine, :] = total

        gat_copies = []
        for d in range(1, chips):
            copy = pltpu.make_async_remote_copy(
                src_ref=gathered.at[t, mine], dst_ref=gathered.at[t, mine],
                send_sem=gat_send.at[t, d - 1], recv_sem=gat_sem.at[t, d - 1],
                device_id=device(chip_ahead(d), core))
            copy.start()
            gat_copies.append(copy)
        fwd_copies = []
        for d in range(chips):
            if d > 0:
                gat_copies[d - 1].wait_recv()
            rows = row_of(core, chip_behind(d))
            copy = pltpu.make_async_remote_copy(
                src_ref=gathered.at[t, rows], dst_ref=gathered.at[t, rows],
                send_sem=fwd_send.at[t, d], recv_sem=fwd_sem.at[t, d],
                device_id=device(chip, other))
            copy.start()
            fwd_copies.append(copy)
        for copy in fwd_copies:
            copy.wait_recv()
        for copy in [core_copy] + part_copies + gat_copies + fwd_copies:
            copy.wait_send()

    acc[...] = jnp.zeros_like(acc)

    @pl.loop(0, chunks)
    def _(i):
        cols = pl.ds(pl.multiple_of(i * CHUNK, CHUNK), CHUNK)
        e_copy(i).wait()
        e = e_buf[:, cols]
        boltz = jnp.exp(jnp.min(e, axis=0, keepdims=True) - e).astype(jnp.bfloat16)
        bz[:, cols] = boltz
        boltz_t = boltz.T
        bzt[cols, :] = boltz_t
        m_copy(i).wait()
        terms(i, boltz, boltz_t)

    pl.semaphore_wait(barrier, chips)

    for t in range(ITERS):
        all_reduce(t)
        if t < ITERS - 1:
            weight[...] = (counts[...] * (gathered[t, 0:1, :] / gathered[t])).astype(jnp.bfloat16)
            acc[...] = jnp.zeros_like(acc)

            @pl.loop(0, chunks)
            def _(i):
                cols = pl.ds(pl.multiple_of(i * CHUNK, CHUNK), CHUNK)
                terms(i, bz[:, cols], bzt[cols, :])

    out_ref[...] = gathered[ITERS - 1]


def on_device(num_dev, energies, mult, state_counts):
    states, samples = energies.shape
    reps = mult.shape[1]
    chips = num_dev // 2
    chunks = samples // CHUNK
    hrows = states // 2
    f32, bf16 = jnp.float32, jnp.bfloat16
    dma = pltpu.SemaphoreType.DMA
    totals = pl.pallas_call(
        functools.partial(mbar_kernel, num_dev),
        out_shape=jax.ShapeDtypeStruct((states, reps), f32),
        in_specs=[
            pl.BlockSpec(memory_space=pltpu.VMEM),
            pl.BlockSpec(memory_space=pl.ANY),
            pl.BlockSpec(memory_space=pl.ANY),
        ],
        out_specs=pl.BlockSpec(memory_space=pltpu.VMEM),
        scratch_shapes=[
            pltpu.VMEM((states, samples), f32),
            pltpu.VMEM((samples, reps), jnp.int32),
            pltpu.VMEM((states, samples), bf16),
            pltpu.VMEM((samples, states), bf16),
            pltpu.VMEM((states, reps), bf16),
            pltpu.VMEM((states, reps), f32),
            pltpu.VMEM((states, reps), f32),
            pltpu.VMEM((ITERS, hrows, reps), f32),
            pltpu.VMEM((ITERS, hrows, reps), f32),
            pltpu.VMEM((ITERS, chips - 1, hrows // chips, reps), f32),
            pltpu.VMEM((ITERS, states, reps), f32),
            dma((chunks,)),
            dma((chunks,)),
            dma((ITERS, 2)),
            dma((ITERS, chips - 1)),
            dma((ITERS, chips - 1)),
            dma((ITERS, chips - 1)),
            dma((ITERS, chips - 1)),
            dma((ITERS, chips)),
            dma((ITERS, chips)),
        ],
        compiler_params=pltpu.CompilerParams(
            collective_id=0, has_side_effects=True, vmem_limit_bytes=56 * 1024 * 1024
        ),
        cost_estimate=pl.CostEstimate(
            flops=4 * ITERS * states * samples * reps,
            bytes_accessed=4 * samples * (states + reps),
            transcendentals=states * samples,
        ),
    )(state_counts.reshape(1, states), energies, mult)
    logs = jnp.log(totals)
    return logs[0:1] - logs


def solution(mesh):
    in_specs = (P(None, ("groups", "samples")), P(("groups", "samples"), None), P("groups"))
    out_specs = P("groups", None)
    return jax.shard_map(
        functools.partial(on_device, mesh.shape["samples"]),
        mesh=mesh, in_specs=in_specs, out_specs=out_specs, check_vma=False,
    )
```

```python
import functools

import jax
import jax.numpy as jnp
from jax import lax
from jax.experimental import pallas as pl
from jax.experimental.pallas import tpu as pltpu
from jax.sharding import PartitionSpec as P

ITERS = 4
CHUNK = 2048
BIG = 6144


def mbar_kernel(num_dev, counts_ref, e_hbm, m_hbm, out_ref, e_buf, m_buf, bz, bzt, weight,
                counts, acc, half, core_recv, part_recv, gathered,
                e_sem, m_sem, core_send, core_sem, part_send, part_sem, gat_send, gat_sem, fwd_send, fwd_sem):
    states, reps = acc.shape
    samples = e_buf.shape[1]
    chunks = samples // CHUNK
    chips = num_dev // 2
    hrows = states // 2
    prows = hrows // chips
    me = lax.axis_index("samples")
    chip, core = me // 2, lax.rem(me, 2)
    other = 1 - core

    def device(chip_at, core_at):
        return {"samples": chip_at * 2 + core_at}

    def partner(d):
        return lax.bitwise_xor(chip, d)

    def e_copy(i):
        cols = pl.ds(pl.multiple_of(i * CHUNK, CHUNK), CHUNK)
        return pltpu.make_async_copy(e_hbm.at[:, cols], e_buf.at[:, cols], e_sem.at[i])

    def m_copy(i):
        rows = pl.ds(pl.multiple_of(i * CHUNK, CHUNK), CHUNK)
        return pltpu.make_async_copy(m_hbm.at[rows, :], m_buf.at[rows, :], m_sem.at[i])

    @pl.loop(0, chunks)
    def _(i):
        e_copy(i).start()
        m_copy(i).start()

    barrier = pltpu.get_barrier_semaphore()
    pl.semaphore_signal(barrier, inc=1, device_id=device(chip, other))
    for d in range(1, chips):
        pl.semaphore_signal(barrier, inc=1, device_id=device(partner(d), core))

    counts[...] = jnp.broadcast_to(counts_ref[...].astype(jnp.float32), (reps, states)).T
    weight[...] = counts[...].astype(jnp.bfloat16)

    def terms(i, boltz, boltz_t, size):
        rows = pl.ds(pl.multiple_of(i * size, size), size)
        denom = jnp.dot(boltz_t, weight[...], preferred_element_type=jnp.float32)
        ratio = (m_buf[rows, :].astype(jnp.float32) / denom).astype(jnp.bfloat16)
        acc[...] += jnp.dot(boltz, ratio, preferred_element_type=jnp.float32)

    def all_reduce(t):
        def part_of(at):
            return pl.ds(pl.multiple_of(at * prows, prows), prows)

        def row_of(core_at, chip_at):
            return pl.ds(pl.multiple_of(core_at * hrows + chip_at * prows, prows), prows)

        order = list(range(chips - 1, -1, -1))
        core_copies = {}
        for d in order:
            to = partner(d)
            copy = pltpu.make_async_remote_copy(
                src_ref=acc.at[row_of(other, to)], dst_ref=core_recv.at[t, part_of(to)],
                send_sem=core_send.at[t, d], recv_sem=core_sem.at[t, d],
                device_id=device(chip, other))
            copy.start()
            core_copies[d] = copy
        part_copies = {}
        for d in range(chips - 1, 0, -1):
            to = partner(d)
            core_copies[d].wait_recv()
            half[t, part_of(to), :] = acc[row_of(core, to), :] + core_recv[t, part_of(to), :]
            copy = pltpu.make_async_remote_copy(
                src_ref=half.at[t, part_of(to)], dst_ref=part_recv.at[t, d - 1],
                send_sem=part_send.at[t, d - 1], recv_sem=part_sem.at[t, d - 1],
                device_id=device(to, core))
            copy.start()
            part_copies[d] = copy
        core_copies[0].wait_recv()
        total = acc[row_of(core, chip), :] + core_recv[t, part_of(chip), :]
        for d in range(1, chips):
            part_copies[d].wait_recv()
            total = total + part_recv[t, d - 1]
        mine = row_of(core, chip)
        gathered[t, mine, :] = total

        gat_copies = {}
        for d in range(chips - 1, 0, -1):
            copy = pltpu.make_async_remote_copy(
                src_ref=gathered.at[t, mine], dst_ref=gathered.at[t, mine],
                send_sem=gat_send.at[t, d - 1], recv_sem=gat_sem.at[t, d - 1],
                device_id=device(partner(d), core))
            copy.start()
            gat_copies[d] = copy
        fwd_copies = []
        for d in range(chips):
            if d > 0:
                gat_copies[d].wait_recv()
            rows = row_of(core, partner(d))
            copy = pltpu.make_async_remote_copy(
                src_ref=gathered.at[t, rows], dst_ref=gathered.at[t, rows],
                send_sem=fwd_send.at[t, d], recv_sem=fwd_sem.at[t, d],
                device_id=device(chip, other))
            copy.start()
            fwd_copies.append(copy)
        for copy in fwd_copies:
            copy.wait_recv()
        for copy in [*core_copies.values(), *part_copies.values(), *gat_copies.values(), *fwd_copies]:
            copy.wait_send()

    acc[...] = jnp.zeros_like(acc)

    @pl.loop(0, chunks)
    def _(i):
        cols = pl.ds(pl.multiple_of(i * CHUNK, CHUNK), CHUNK)
        e_copy(i).wait()
        e = e_buf[:, cols]
        boltz = jnp.exp(jnp.min(e, axis=0, keepdims=True) - e).astype(jnp.bfloat16)
        bz[:, cols] = boltz
        boltz_t = boltz.T
        bzt[cols, :] = boltz_t
        m_copy(i).wait()
        terms(i, boltz, boltz_t, CHUNK)

    pl.semaphore_wait(barrier, chips)

    for t in range(ITERS):
        all_reduce(t)
        if t < ITERS - 1:
            weight[...] = (counts[...] * (gathered[t, 0:1, :] / gathered[t])).astype(jnp.bfloat16)
            acc[...] = jnp.zeros_like(acc)

            @pl.loop(0, samples // BIG)
            def _(i):
                cols = pl.ds(pl.multiple_of(i * BIG, BIG), BIG)
                terms(i, bz[:, cols], bzt[cols, :], BIG)

    out_ref[...] = gathered[ITERS - 1]


def on_device(num_dev, energies, mult, state_counts):
    states, samples = energies.shape
    reps = mult.shape[1]
    chips = num_dev // 2
    chunks = samples // CHUNK
    hrows = states // 2
    f32, bf16 = jnp.float32, jnp.bfloat16
    dma = pltpu.SemaphoreType.DMA
    totals = pl.pallas_call(
        functools.partial(mbar_kernel, num_dev),
        out_shape=jax.ShapeDtypeStruct((states, reps), f32),
        in_specs=[
            pl.BlockSpec(memory_space=pltpu.VMEM),
            pl.BlockSpec(memory_space=pl.ANY),
            pl.BlockSpec(memory_space=pl.ANY),
        ],
        out_specs=pl.BlockSpec(memory_space=pltpu.VMEM),
        scratch_shapes=[
            pltpu.VMEM((states, samples), f32),
            pltpu.VMEM((samples, reps), jnp.int32),
            pltpu.VMEM((states, samples), bf16),
            pltpu.VMEM((samples, states), bf16),
            pltpu.VMEM((states, reps), bf16),
            pltpu.VMEM((states, reps), f32),
            pltpu.VMEM((states, reps), f32),
            pltpu.VMEM((ITERS, hrows, reps), f32),
            pltpu.VMEM((ITERS, hrows, reps), f32),
            pltpu.VMEM((ITERS, chips - 1, hrows // chips, reps), f32),
            pltpu.VMEM((ITERS, states, reps), f32),
            dma((chunks,)),
            dma((chunks,)),
            dma((ITERS, chips)),
            dma((ITERS, chips)),
            dma((ITERS, chips - 1)),
            dma((ITERS, chips - 1)),
            dma((ITERS, chips - 1)),
            dma((ITERS, chips - 1)),
            dma((ITERS, chips)),
            dma((ITERS, chips)),
        ],
        compiler_params=pltpu.CompilerParams(
            collective_id=0, has_side_effects=True, vmem_limit_bytes=56 * 1024 * 1024
        ),
        cost_estimate=pl.CostEstimate(
            flops=4 * ITERS * states * samples * reps,
            bytes_accessed=4 * samples * (states + reps),
            transcendentals=states * samples,
        ),
    )(state_counts.reshape(1, states), energies, mult)
    logs = jnp.log(totals)
    return logs[0:1] - logs


def solution(mesh):
    in_specs = (P(None, ("groups", "samples")), P(("groups", "samples"), None), P("groups"))
    out_specs = P("groups", None)
    return jax.shard_map(
        functools.partial(on_device, mesh.shape["samples"]),
        mesh=mesh, in_specs=in_specs, out_specs=out_specs, check_vma=False,
    )
```
